32 devices in a mesh: sec: 4 (over y, core), blk: 8 (over z, x).
Axes of the slice: x: 2, y: 2, z: 4, core: 2. Of those that a mesh axis runs over, the one named last changes fastest.
Arguments:
- left_built: bfloat16 [4, 6, 16, 256, 256], P('sec', None, 'blk'), may hold values from -0.375 to 0.375
- right_env: bfloat16 [4, 6, 16, 256, 256], P('sec', None, 'blk'), may hold values from -0.375 to 0.375
- psi_init: float32 [4, 16, 256, 256], P('sec', 'blk')
- block_dims: int32 [4, 16], P('sec', 'blk'), may hold values from 64 to 256, as said below
- ranks: int32 [4, 16], P('sec', 'blk'), may hold values from 2 to 128, as said below
- sketch: float32 [4, 16, 256, 128], P('sec', 'blk'), may hold values from -6 to 6
Outputs:
- truncated: float32 [4, 16, 256, 256], P('sec', 'blk')
- alphas: float32 [4, 4], P('sec')
- betas: float32 [4, 4], P('sec')
The draws below stay inside these ranges and needn't reach their ends.
Inputs may be any that keep to these rules, and one draw needn't show every extreme that they name: `block_dims`: in each section at least one block has dimension exactly 256. `ranks`: each rank is at most half of its block's dimension; in each section at least one block of dimension 256 has rank 256 // 2.
All inputs are finite; a program needn't handle non-finite values.
Results may differ from the reference program's by a relative error of at most 0.0096.
Values may be sent and summed in bfloat16 or wider, within the bound.
A program may use at most 64 MiB of HBM per device.

```python
import jax
import jax.numpy as jnp
from jax import lax

B = 256
W = 6
NB = 2
STEPS = 4
RMAX = 128
SECTORS = 16
N_SEC = 4


def sector_table(key):
    keys = jax.random.split(jax.random.fold_in(key, 11), 3)
    dims = jax.random.randint(keys[0], (N_SEC, SECTORS), B // 4, B + 1)
    pick = jax.random.randint(keys[1], (N_SEC,), 0, SECTORS)
    hit = jnp.arange(SECTORS)[None, :] == pick[:, None]
    dims = jnp.where(hit, B, dims)
    ranks = jax.random.randint(keys[2], (N_SEC, SECTORS), 2, dims // 2 + 1)
    ranks = jnp.where(hit, B // 2, ranks)
    return (dims.astype(jnp.int32), ranks.astype(jnp.int32))


def draw_block_dims(key, part):
    return sector_table(key)[0]


def draw_ranks(key, part):
    return sector_table(key)[1]


def draw_psi_init(key, part):
    keys = jax.random.split(jax.random.fold_in(key, 23), 1)
    ramp = 3.0 ** (jnp.arange(SECTORS, dtype=jnp.float32) / max(SECTORS - 1, 1))
    ramp = ramp[None, :, None, None]
    base = jax.random.normal(keys[0], (N_SEC, SECTORS, B, B), jnp.float32)
    return (base * ramp).astype(jnp.float32)


def shard_levels(own_key, shape, shards, low, largest):
    level, own = 1.0, jax.random.fold_in(own_key, 6)
    for dim, shards_of in shards:
        draws = jnp.exp(jax.random.uniform(jax.random.fold_in(own, dim), (shards_of,), jnp.float32, low / len(shards), largest / len(shards)))
        level = level * jnp.repeat(draws, shape[dim] // shards_of).reshape([-1 if axis == dim else 1 for axis in range(len(shape))])
    return level


def noise(key, shape, spread, limit, cuts=(), kind=jnp.bfloat16):
    level = shard_levels(key, shape, cuts, -0.22, 0.18) if cuts else 1.0
    result = jax.random.normal(key, shape, jnp.float32) * spread * level
    return jnp.minimum(jnp.maximum(result, -limit), limit).astype(kind)


def setup_inputs(seed: int = 0) -> dict:
    seeds = jax.random.split(jax.random.key(seed), 7)
    left_built = noise(seeds[0], (N_SEC, W, SECTORS, B, B), B ** -0.5, 0.375, ((0, 4), (2, 8)))
    right_env = noise(seeds[1], (N_SEC, W, SECTORS, B, B), B ** -0.5, 0.375, ((0, 4), (2, 8)))
    psi_init = draw_psi_init(jax.random.fold_in(seeds[6], 71), 0)
    block_dims = draw_block_dims(jax.random.fold_in(seeds[6], 71), 0)
    ranks = draw_ranks(jax.random.fold_in(seeds[6], 71), 0)
    sketch = noise(seeds[5], (N_SEC, SECTORS, B, RMAX), 1.0, 6.0, ((0, 4), (1, 8)), jnp.float32)
    return dict(left_built=left_built, right_env=right_env, psi_init=psi_init, block_dims=block_dims, ranks=ranks, sketch=sketch)


def apply_ham(vbf, left, right, cellmask, spin_low, spin_high):
    vals = lax.optimization_barrier(vbf).astype(jnp.float32)
    width = NB + 1
    padded = jnp.pad(vals, ((width, width), (0, 0), (0, 0)))
    sources = [vals, vals, padded[1:1 + SECTORS], padded[2 * NB + 1:2 * NB + 1 + SECTORS], padded[0:SECTORS] * spin_low, padded[2 * NB + 2:2 * NB + 2 + SECTORS] * spin_high]
    total = jnp.zeros(vals.shape, jnp.float32)
    for k in range(W):
        mixed = jnp.einsum('qab,qcb->qac', sources[k], right[k].astype(jnp.float32))
        mixed = lax.optimization_barrier(mixed.astype(jnp.bfloat16)).astype(jnp.float32)
        total = total + jnp.einsum('qab,qbc->qac', left[k].astype(jnp.float32), mixed)
    return total * cellmask

def project_block(blockv, sketchb, cmask):
    hp = lax.Precision.HIGHEST
    ymat = jnp.dot(blockv, sketchb, precision=hp) * cmask[None, :]
    gram = jnp.dot(ymat.T, ymat, precision=hp) + jnp.diag(1.0 - cmask)
    factor = jnp.linalg.cholesky(gram)
    rhs = jnp.dot(ymat.T, blockv, precision=hp)
    inner = lax.linalg.triangular_solve(factor, rhs, left_side=True, lower=True)
    coef = lax.linalg.triangular_solve(factor, inner, left_side=True, lower=True, transpose_a=True)
    return jnp.dot(ymat, coef, precision=hp)

def one_section(inputs):
    left, right, start, dims, rank_row, sketch_sec = inputs
    iota = jnp.arange(B)
    rowmask = (iota[None, :] < dims[:, None]).astype(jnp.float32)
    cellmask = rowmask[:, :, None] * rowmask[:, None, :]
    spin = jnp.arange(SECTORS) % NB
    spin_low = (spin >= 1).astype(jnp.float32)[:, None, None]
    spin_high = (spin <= NB - 2).astype(jnp.float32)[:, None, None]
    count = float(SECTORS * B * B)
    vec = start * cellmask
    vec = vec * jnp.sqrt(count / jnp.sum(vec * vec))
    prev = jnp.zeros_like(vec)
    beta = jnp.float32(0.0)
    alpha_list = []
    beta_list = []
    for step in range(STEPS):
        image = apply_ham(vec.astype(jnp.bfloat16), left, right, cellmask, spin_low, spin_high)
        alpha = jnp.sum(vec * image) / count
        resid = image - alpha * vec - beta * prev
        beta = jnp.sqrt(jnp.sum(resid * resid) / count + 1e-06)
        prev = vec
        vec = resid / beta
        alpha_list.append(alpha)
        beta_list.append(beta)
    cmask = (jnp.arange(B // 2)[None, :] < rank_row[:, None]).astype(jnp.float32)
    cut_off = jax.vmap(project_block)(vec, sketch_sec, cmask)
    return (cut_off, jnp.stack(alpha_list), jnp.stack(beta_list))

def reference(left_built, right_env, psi_init, block_dims, ranks, sketch):
    left_all = jnp.roll(left_built, 1, axis=0)
    return lax.map(one_section, (left_all, right_env, psi_init, block_dims, ranks, sketch))
```

```python
import functools

import jax
import jax.numpy as jnp
from jax import lax
from jax.experimental import pallas as pl
from jax.experimental.pallas import tpu as pltpu
from jax.sharding import PartitionSpec as P

STEPS = 4
MESH = pl.DeviceIdType.MESH


def lanczos_kernel(
    n, nsec, count, dims_ref, left_ref, right_ref, psi_ref, vec_ref, coef_ref,
    left, own, low, high, prev, image, mask, mixed, row, rows, beta_ref,
    left_send, left_recv, halo_send, halo_recv, row_send, row_recv,
):
    blocks, side = psi_ref.shape[0], psi_ref.shape[1]
    terms = right_ref.shape[0]
    me = lax.axis_index("blk")
    sec = lax.axis_index("sec")
    after = lax.rem(sec + 1, nsec)
    before = lax.rem(sec + nsec - 1, nsec)

    barrier = pltpu.get_barrier_semaphore()

    def greet(o, carry):
        pl.semaphore_signal(barrier, inc=1, device_id={"blk": lax.rem(me + o, n)}, device_id_type=MESH)
        return carry

    lax.fori_loop(1, n, greet, 0)
    for other in (after, before):
        pl.semaphore_signal(barrier, inc=1, device_id={"sec": other}, device_id_type=MESH)
    pl.semaphore_wait(barrier, n + 1)

    left_copy = pltpu.make_async_remote_copy(
        src_ref=left_ref, dst_ref=left, send_sem=left_send, recv_sem=left_recv,
        device_id={"sec": after}, device_id_type=MESH,
    )
    left_copy.start()

    def row_copy(r, o, slot, target):
        return pltpu.make_async_remote_copy(
            src_ref=row.at[r], dst_ref=rows.at[r, slot],
            send_sem=row_send.at[r, o], recv_sem=row_recv.at[r, o],
            device_id={"blk": target}, device_id_type=MESH,
        )

    def exchange(r, sums):
        line = lax.broadcasted_iota(jnp.int32, (8, 128), 0)
        tile = jnp.zeros((8, 128), jnp.float32)
        for i, s in enumerate(sums):
            tile = jnp.where(line == i, s, tile)
        row[r] = tile
        rows[r, me] = tile

        def send(o, carry):
            row_copy(r, o, me, lax.rem(me + o, n)).start()
            return carry

        def take(o, carry):
            row_copy(r, o, lax.rem(me + n - o, n), lax.rem(me + o, n)).wait_recv()
            return carry

        lax.fori_loop(1, n, send, 0)
        lax.fori_loop(1, n, take, 0)
        return rows[r]

    def drain(r):
        def sent(o, carry):
            row_copy(r, o, me, lax.rem(me + o, n)).wait_send()
            return carry

        lax.fori_loop(1, n, sent, 0)

    def dot2(a, b):
        return jnp.sum(jnp.sum(a * b, axis=0), axis=(0, 1), keepdims=True)

    for q in range(blocks):
        d = dims_ref[q]
        inside = (lax.broadcasted_iota(jnp.int32, (side, side), 0) < d) & (
            lax.broadcasted_iota(jnp.int32, (side, side), 1) < d
        )
        mask[q] = inside.astype(jnp.float32)

    vec_ref[...] = psi_ref[...] * mask[...]
    prev[...] = jnp.zeros_like(prev)
    beta_ref[...] = jnp.zeros_like(beta_ref)

    @pl.when(me == 0)
    def _():
        low[...] = jnp.zeros_like(low)

    @pl.when(me == n - 1)
    def _():
        high[...] = jnp.zeros_like(high)

    got = exchange(0, [dot2(vec_ref[...], vec_ref[...])])
    start_sq = jnp.sum(got[:, 0:1, :], axis=0)[:, :1]
    vec_ref[...] = vec_ref[...] * jnp.sqrt(count / start_sq)
    drain(0)

    def step_body(step, carry):
        own[step] = vec_ref[...].astype(jnp.bfloat16)
        up = pltpu.make_async_remote_copy(
            src_ref=own.at[step], dst_ref=low.at[step],
            send_sem=halo_send.at[step, 0], recv_sem=halo_recv.at[step, 0],
            device_id={"blk": lax.rem(me + 1, n)}, device_id_type=MESH,
        )
        down = pltpu.make_async_remote_copy(
            src_ref=own.at[step], dst_ref=high.at[step],
            send_sem=halo_send.at[step, 1], recv_sem=halo_recv.at[step, 1],
            device_id={"blk": lax.rem(me + n - 1, n)}, device_id_type=MESH,
        )

        @pl.when(me < n - 1)
        def _():
            up.start()

        @pl.when(me > 0)
        def _():
            down.start()

        def mix(k, q, source):
            mixed[k, q] = lax.dot_general(
                source, right_ref[k, q], (((1,), (1,)), ((), ())), preferred_element_type=jnp.float32
            ).astype(jnp.bfloat16)

        def apply(ks, q):
            total = None
            for k in ks:
                part = jnp.dot(left[k, q], mixed[k, q], preferred_element_type=jnp.float32)
                total = part if total is None else total + part
            return total

        for q in range(blocks):
            mix(0, q, own[step, q])
            mix(1, q, own[step, q])

        @pl.when(me > 0)
        def _():
            up.wait_recv()

        @pl.when(me < n - 1)
        def _():
            down.wait_recv()

        for q in range(blocks):
            mix(2, q, low[step, q])
            mix(3, q, high[step, q])
            if q > 0:
                mix(4, q, low[step, q - 1])
            if q < blocks - 1:
                mix(5, q, high[step, q + 1])

        @pl.when(step == 0)
        def _():
            left_copy.wait()

        for q in range(blocks):
            ks = [0, 1, 2, 3] + ([4] if q > 0 else []) + ([5] if q < blocks - 1 else [])
            image[q] = apply(ks, q) * mask[q]

        beta = beta_ref[0:1, 0:1]
        vec = vec_ref[...]
        vw = dot2(vec, image[...])
        vv = dot2(vec, vec)
        image[...] = image[...] - beta * prev[...]
        vt = dot2(vec, image[...])
        mine = vt / jnp.where(vv > 0.0, vv, 1.0)
        rest = image[...] - mine * vec
        got = exchange(step + 1, [vw, mine, vv, dot2(rest, rest), dot2(rest, vec)])
        alpha = jnp.sum(got[:, 0:1, :], axis=0) / count
        gap = got[:, 1:2, :] - alpha[None]
        resid = jnp.sum(got[:, 3:4, :] + 2.0 * gap * got[:, 4:5, :] + gap * gap * got[:, 2:3, :], axis=0)
        next_beta = jnp.sqrt(jnp.maximum(resid, 0.0) / count + 1e-06)
        coef_ref[pl.ds(step, 1)] = alpha
        coef_ref[pl.ds(STEPS + step, 1)] = next_beta
        beta_ref[0:1] = next_beta
        vec = vec_ref[...]
        fresh = (image[...] - alpha[:, :1] * vec) * (1.0 / next_beta[:, :1])
        prev[...] = vec
        vec_ref[...] = fresh
        drain(step + 1)

        @pl.when(me < n - 1)
        def _():
            up.wait_send()

        @pl.when(me > 0)
        def _():
            down.wait_send()

        return carry

    lax.fori_loop(0, STEPS, step_body, 0)


def lanczos(left_built, right, psi, dims, n, nsec):
    blocks, side = psi.shape[0], psi.shape[1]
    terms = right.shape[0]
    count = float(n * blocks * side * side)
    vmem = pl.BlockSpec(memory_space=pltpu.VMEM)
    half = jnp.bfloat16
    return pl.pallas_call(
        functools.partial(lanczos_kernel, n, nsec, count),
        out_shape=(
            jax.ShapeDtypeStruct((blocks, side, side), jnp.float32),
            jax.ShapeDtypeStruct((2 * STEPS, 128), jnp.float32),
        ),
        in_specs=[pl.BlockSpec(memory_space=pltpu.SMEM), pl.BlockSpec(memory_space=pl.ANY), vmem, vmem],
        out_specs=(vmem, vmem),
        scratch_shapes=[
            pltpu.VMEM((terms, blocks, side, side), half),
            pltpu.VMEM((STEPS, blocks, side, side), half),
            pltpu.VMEM((STEPS, blocks, side, side), half),
            pltpu.VMEM((STEPS, blocks, side, side), half),
            pltpu.VMEM((blocks, side, side), jnp.float32),
            pltpu.VMEM((blocks, side, side), jnp.float32),
            pltpu.VMEM((blocks, side, side), jnp.float32),
            pltpu.VMEM((terms, blocks, side, side), half),
            pltpu.VMEM((STEPS + 1, 8, 128), jnp.float32),
            pltpu.VMEM((STEPS + 1, n, 8, 128), jnp.float32),
            pltpu.VMEM((8, 128), jnp.float32),
            pltpu.SemaphoreType.DMA,
            pltpu.SemaphoreType.DMA,
            pltpu.SemaphoreType.DMA((STEPS, 2)),
            pltpu.SemaphoreType.DMA((STEPS, 2)),
            pltpu.SemaphoreType.DMA((STEPS + 1, n)),
            pltpu.SemaphoreType.DMA((STEPS + 1, n)),
        ],
        compiler_params=pltpu.CompilerParams(
            collective_id=0, has_side_effects=True, vmem_limit_bytes=40 * 1024 * 1024
        ),
        name="lanczos",
    )(dims, left_built, right, psi)


def project_block(blockv, sketchb, cmask):
    hp = lax.Precision.HIGHEST
    ymat = jnp.dot(blockv, sketchb, precision=hp) * cmask[None, :]
    gram = jnp.dot(ymat.T, ymat, precision=hp) + jnp.diag(1.0 - cmask)
    factor = jnp.linalg.cholesky(gram)
    rhs = jnp.dot(ymat.T, blockv, precision=hp)
    inner = lax.linalg.triangular_solve(factor, rhs, left_side=True, lower=True)
    coef = lax.linalg.triangular_solve(factor, inner, left_side=True, lower=True, transpose_a=True)
    return jnp.dot(ymat, coef, precision=hp)


def shards(left_built, right_env, psi_init, block_dims, ranks, sketch):
    n = lax.axis_size("blk")
    nsec = lax.axis_size("sec")
    vec, coefs = lanczos(left_built[0], right_env[0], psi_init[0], block_dims[0], n, nsec)
    rmax = sketch.shape[3]
    cmask = (jnp.arange(rmax)[None, :] < ranks[0][:, None]).astype(jnp.float32)
    truncated = jax.vmap(project_block)(vec, sketch[0], cmask)
    return (truncated[None], coefs[:STEPS, 0][None], coefs[STEPS:, 0][None])


def solution(mesh):
    placed = (
        P("sec", None, "blk", None, None),
        P("sec", None, "blk", None, None),
        P("sec", "blk", None, None),
        P("sec", "blk"),
        P("sec", "blk"),
        P("sec", "blk", None, None),
    )
    return jax.shard_map(
        shards,
        mesh=mesh,
        in_specs=placed,
        out_specs=(P("sec", "blk", None, None), P("sec", None), P("sec", None)),
        check_vma=False,
    )
```

```python
import functools

import jax
import jax.numpy as jnp
from jax import lax
from jax.experimental import pallas as pl
from jax.experimental.pallas import tpu as pltpu
from jax.sharding import PartitionSpec as P

STEPS = 4
MESH = pl.DeviceIdType.MESH


def lanczos_kernel(
    n, nsec, count, dims_ref, left_ref, right_ref, psi_ref, vec_ref, coef_ref,
    left, own, low, high, prev, image, mask, mixed, row, rows, beta_ref,
    left_send, left_recv, halo_send, halo_recv, row_send, row_recv,
):
    blocks, side = psi_ref.shape[0], psi_ref.shape[1]
    terms = right_ref.shape[0]
    me = lax.axis_index("blk")
    sec = lax.axis_index("sec")
    after = lax.rem(sec + 1, nsec)
    before = lax.rem(sec + nsec - 1, nsec)

    barrier = pltpu.get_barrier_semaphore()

    def greet(o, carry):
        pl.semaphore_signal(barrier, inc=1, device_id={"blk": lax.rem(me + o, n)}, device_id_type=MESH)
        return carry

    lax.fori_loop(1, n, greet, 0)
    for other in (after, before):
        pl.semaphore_signal(barrier, inc=1, device_id={"sec": other}, device_id_type=MESH)
    pl.semaphore_wait(barrier, n + 1)

    left_copy = pltpu.make_async_remote_copy(
        src_ref=left_ref, dst_ref=left, send_sem=left_send, recv_sem=left_recv,
        device_id={"sec": after}, device_id_type=MESH,
    )
    left_copy.start()

    def row_copy(r, o, slot, target):
        return pltpu.make_async_remote_copy(
            src_ref=row.at[r], dst_ref=rows.at[r, slot],
            send_sem=row_send.at[r, o], recv_sem=row_recv.at[r, o],
            device_id={"blk": target}, device_id_type=MESH,
        )

    def exchange(r, sums):
        line = lax.broadcasted_iota(jnp.int32, (8, 128), 0)
        tile = jnp.zeros((8, 128), jnp.float32)
        for i, s in enumerate(sums):
            tile = jnp.where(line == i, s, tile)
        row[r] = tile
        rows[r, me] = tile

        def send(o, carry):
            row_copy(r, o, me, lax.rem(me + o, n)).start()
            return carry

        def take(o, carry):
            row_copy(r, o, lax.rem(me + n - o, n), lax.rem(me + o, n)).wait_recv()
            return carry

        lax.fori_loop(1, n, send, 0)
        lax.fori_loop(1, n, take, 0)
        return rows[r]

    def drain(r):
        def sent(o, carry):
            row_copy(r, o, me, lax.rem(me + o, n)).wait_send()
            return carry

        lax.fori_loop(1, n, sent, 0)

    def dot2(a, b):
        return jnp.sum(jnp.sum(a * b, axis=0), axis=(0, 1), keepdims=True)

    for q in range(blocks):
        d = dims_ref[q]
        inside = (lax.broadcasted_iota(jnp.int32, (side, side), 0) < d) & (
            lax.broadcasted_iota(jnp.int32, (side, side), 1) < d
        )
        mask[q] = inside.astype(jnp.float32)

    vec_ref[...] = psi_ref[...] * mask[...]
    prev[...] = jnp.zeros_like(prev)
    beta_ref[...] = jnp.zeros_like(beta_ref)

    @pl.when(me == 0)
    def _():
        low[...] = jnp.zeros_like(low)

    @pl.when(me == n - 1)
    def _():
        high[...] = jnp.zeros_like(high)

    got = exchange(0, [dot2(vec_ref[...], vec_ref[...])])
    start_sq = jnp.sum(got[:, 0:1, :], axis=0)[:, :1]
    vec_ref[...] = vec_ref[...] * jnp.sqrt(count / start_sq)
    drain(0)

    def step_body(step, carry):
        own[step] = vec_ref[...].astype(jnp.bfloat16)
        up = pltpu.make_async_remote_copy(
            src_ref=own.at[step], dst_ref=low.at[step],
            send_sem=halo_send.at[step, 0], recv_sem=halo_recv.at[step, 0],
            device_id={"blk": lax.rem(me + 1, n)}, device_id_type=MESH,
        )
        down = pltpu.make_async_remote_copy(
            src_ref=own.at[step], dst_ref=high.at[step],
            send_sem=halo_send.at[step, 1], recv_sem=halo_recv.at[step, 1],
            device_id={"blk": lax.rem(me + n - 1, n)}, device_id_type=MESH,
        )

        @pl.when(me < n - 1)
        def _():
            up.start()

        @pl.when(me > 0)
        def _():
            down.start()

        def mix(k, q, source):
            mixed[k, q] = lax.dot_general(
                source, right_ref[k, q], (((1,), (1,)), ((), ())), preferred_element_type=jnp.float32
            ).astype(jnp.bfloat16)

        def apply(ks, q):
            total = None
            for k in ks:
                part = jnp.dot(left[k, q], mixed[k, q], preferred_element_type=jnp.float32)
                total = part if total is None else total + part
            return total

        for q in range(blocks):
            mix(0, q, own[step, q])
            mix(1, q, own[step, q])

        @pl.when(me > 0)
        def _():
            up.wait_recv()

        @pl.when(me < n - 1)
        def _():
            down.wait_recv()

        for q in range(blocks):
            mix(2, q, low[step, q])
            mix(3, q, high[step, q])
            if q > 0:
                mix(4, q, low[step, q - 1])
            if q < blocks - 1:
                mix(5, q, high[step, q + 1])

        @pl.when(step == 0)
        def _():
            left_copy.wait()

        for q in range(blocks):
            ks = [0, 1, 2, 3] + ([4] if q > 0 else []) + ([5] if q < blocks - 1 else [])
            image[q] = apply(ks, q) * mask[q]

        beta = beta_ref[0:1, 0:1]
        vec = vec_ref[...]
        vw = dot2(vec, image[...])
        vv = dot2(vec, vec)
        image[...] = image[...] - beta * prev[...]
        vt = dot2(vec, image[...])
        mine = vt / jnp.where(vv > 0.0, vv, 1.0)
        rest = image[...] - mine * vec
        got = exchange(step + 1, [vw, mine, vv, dot2(rest, rest), dot2(rest, vec)])
        alpha = jnp.sum(got[:, 0:1, :], axis=0) / count
        gap = got[:, 1:2, :] - alpha[None]
        resid = jnp.sum(got[:, 3:4, :] + 2.0 * gap * got[:, 4:5, :] + gap * gap * got[:, 2:3, :], axis=0)
        next_beta = jnp.sqrt(jnp.maximum(resid, 0.0) / count + 1e-06)
        coef_ref[pl.ds(step, 1)] = alpha
        coef_ref[pl.ds(STEPS + step, 1)] = next_beta
        beta_ref[0:1] = next_beta
        vec = vec_ref[...]
        fresh = (image[...] - alpha[:, :1] * vec) * (1.0 / next_beta[:, :1])
        prev[...] = vec
        vec_ref[...] = fresh
        drain(step + 1)

        @pl.when(me < n - 1)
        def _():
            up.wait_send()

        @pl.when(me > 0)
        def _():
            down.wait_send()

        return carry

    lax.fori_loop(0, STEPS, step_body, 0)


def lanczos(left_built, right, psi, dims, n, nsec):
    blocks, side = psi.shape[0], psi.shape[1]
    terms = right.shape[0]
    count = float(n * blocks * side * side)
    vmem = pl.BlockSpec(memory_space=pltpu.VMEM)
    half = jnp.bfloat16
    return pl.pallas_call(
        functools.partial(lanczos_kernel, n, nsec, count),
        out_shape=(
            jax.ShapeDtypeStruct((blocks, side, side), jnp.float32),
            jax.ShapeDtypeStruct((2 * STEPS, 128), jnp.float32),
        ),
        in_specs=[pl.BlockSpec(memory_space=pltpu.SMEM), pl.BlockSpec(memory_space=pl.ANY), vmem, vmem],
        out_specs=(vmem, vmem),
        scratch_shapes=[
            pltpu.VMEM((terms, blocks, side, side), half),
            pltpu.VMEM((STEPS, blocks, side, side), half),
            pltpu.VMEM((STEPS, blocks, side, side), half),
            pltpu.VMEM((STEPS, blocks, side, side), half),
            pltpu.VMEM((blocks, side, side), jnp.float32),
            pltpu.VMEM((blocks, side, side), jnp.float32),
            pltpu.VMEM((blocks, side, side), jnp.float32),
            pltpu.VMEM((terms, blocks, side, side), half),
            pltpu.VMEM((STEPS + 1, 8, 128), jnp.float32),
            pltpu.VMEM((STEPS + 1, n, 8, 128), jnp.float32),
            pltpu.VMEM((8, 128), jnp.float32),
            pltpu.SemaphoreType.DMA,
            pltpu.SemaphoreType.DMA,
            pltpu.SemaphoreType.DMA((STEPS, 2)),
            pltpu.SemaphoreType.DMA((STEPS, 2)),
            pltpu.SemaphoreType.DMA((STEPS + 1, n)),
            pltpu.SemaphoreType.DMA((STEPS + 1, n)),
        ],
        compiler_params=pltpu.CompilerParams(
            collective_id=0, has_side_effects=True, vmem_limit_bytes=40 * 1024 * 1024
        ),
        name="lanczos",
    )(dims, left_built, right, psi)


def project_kernel(ranks_ref, vec_ref, sketch_ref, out_ref, gram, side_rows):
    blocks, side, rmax = sketch_ref.shape
    hp = lax.Precision.HIGHEST

    def mul(x, y, dims):
        return lax.dot_general(x, y, (dims, ((), ())), precision=hp, preferred_element_type=jnp.float32)

    line = lax.broadcasted_iota(jnp.int32, (rmax, rmax), 0)
    lane = lax.broadcasted_iota(jnp.int32, (rmax, rmax), 1)
    wide = lax.broadcasted_iota(jnp.int32, (rmax, side), 0)
    for q in range(blocks):
        rank = ranks_ref[q]
        yt = mul(sketch_ref[q], vec_ref[q], ((0,), (1,)))
        yt = jnp.where(wide < rank, yt, 0.0)
        side_rows[q] = yt
        extra = jnp.where((line == lane) & (line >= rank), 1.0, 0.0)
        gram[q] = mul(yt, yt, ((1,), (1,))) + extra
    sub = lax.broadcasted_iota(jnp.int32, (8, 1), 0)
    for p in range(0, rmax, 8):
        g = [gram[q, p : p + 8, :] for q in range(blocks)]
        y = [side_rows[q, p : p + 8, :] for q in range(blocks)]
        scale = [jnp.ones((8, 1), jnp.float32) for q in range(blocks)]
        for j in range(8):
            for q in range(blocks):
                pivot = g[q][j : j + 1, p + j : p + j + 1]
                factor = jnp.where(sub > j, g[q][:, p + j : p + j + 1], 0.0) / pivot
                scale[q] = jnp.where(sub == j, pivot, scale[q])
                y[q] = y[q] - factor * y[q][j : j + 1, :]
                g[q] = g[q] - factor * g[q][j : j + 1, :]
        for q in range(blocks):
            norm = 1.0 / jnp.sqrt(scale[q])
            g[q] = g[q] * norm
            y[q] = y[q] * norm
            side_rows[q, p : p + 8, :] = y[q]
        if p + 8 < rmax:
            flip = [g[q].T for q in range(blocks)]
            for i in range(p + 8, rmax, 8):
                for q in range(blocks):
                    gi = gram[q, i : i + 8, :]
                    yi = side_rows[q, i : i + 8, :]
                    for j in range(8):
                        f = flip[q][i : i + 8, j : j + 1]
                        gi = gi - f * g[q][j : j + 1, :]
                        yi = yi - f * y[q][j : j + 1, :]
                    gram[q, i : i + 8, :] = gi
                    side_rows[q, i : i + 8, :] = yi
    for q in range(blocks):
        z = side_rows[q]
        out_ref[q] = mul(z, mul(z, vec_ref[q], ((1,), (0,))), ((0,), (0,)))


def project(vec, sketch, ranks, **kw):
    blocks, side, rmax = sketch.shape
    vmem = pl.BlockSpec(memory_space=pltpu.VMEM)
    return pl.pallas_call(
        project_kernel,
        out_shape=jax.ShapeDtypeStruct((blocks, side, side), jnp.float32),
        in_specs=[pl.BlockSpec(memory_space=pltpu.SMEM), vmem, vmem],
        out_specs=vmem,
        scratch_shapes=[
            pltpu.VMEM((blocks, rmax, rmax), jnp.float32),
            pltpu.VMEM((blocks, rmax, side), jnp.float32),
        ],
        compiler_params=pltpu.CompilerParams(vmem_limit_bytes=32 * 1024 * 1024),
        name="project",
        **kw,
    )(ranks, vec, sketch)


def shards(left_built, right_env, psi_init, block_dims, ranks, sketch):
    n = lax.axis_size("blk")
    nsec = lax.axis_size("sec")
    vec, coefs = lanczos(left_built[0], right_env[0], psi_init[0], block_dims[0], n, nsec)
    truncated = project(vec, sketch[0], ranks[0])
    return (truncated[None], coefs[:STEPS, 0][None], coefs[STEPS:, 0][None])


def solution(mesh):
    placed = (
        P("sec", None, "blk", None, None),
        P("sec", None, "blk", None, None),
        P("sec", "blk", None, None),
        P("sec", "blk"),
        P("sec", "blk"),
        P("sec", "blk", None, None),
    )
    return jax.shard_map(
        shards,
        mesh=mesh,
        in_specs=placed,
        out_specs=(P("sec", "blk", None, None), P("sec", None), P("sec", None)),
        check_vma=False,
    )
```

```python
import functools

import jax
import jax.numpy as jnp
from jax import lax
from jax.experimental import pallas as pl
from jax.experimental.pallas import tpu as pltpu
from jax.sharding import PartitionSpec as P

STEPS = 4
MESH = pl.DeviceIdType.MESH


def lanczos_kernel(
    n, nsec, count, dims_ref, left_ref, right_hbm, psi_hbm, vec_ref, coef_ref,
    left, right_ref, psi_ref, own, near, far, prev, image, mask, mixed, row, rows, beta_ref,
    load, left_send, left_recv, near_send, near_recv, far_send, far_recv, row_send, row_recv,
):
    blocks, side = psi_ref.shape[0], psi_ref.shape[1]
    terms = right_ref.shape[0]
    me = lax.axis_index("blk")
    sec = lax.axis_index("sec")
    after = lax.rem(sec + 1, nsec)
    before = lax.rem(sec + nsec - 1, nsec)

    odd = lax.rem(me, 2)
    partner = me + 1 - 2 * odd
    target = me + 2 - 4 * odd
    source = me - 2 + 4 * odd
    has_target = (target >= 0) & (target < n)
    has_source = (source >= 0) & (source < n)
    half = side // 2
    chunks = [(b, h * half) for b in range(blocks) for h in range(2)]

    psi_load = pltpu.make_async_copy(psi_hbm, psi_ref, load.at[0])
    right_load = pltpu.make_async_copy(right_hbm, right_ref, load.at[1])
    psi_load.start()
    right_load.start()

    barrier = pltpu.get_barrier_semaphore()

    def greet(o, carry):
        pl.semaphore_signal(barrier, inc=1, device_id={"blk": lax.rem(me + o, n)}, device_id_type=MESH)
        return carry

    lax.fori_loop(1, n, greet, 0)
    for other in (after, before):
        pl.semaphore_signal(barrier, inc=1, device_id={"sec": other}, device_id_type=MESH)
    pl.semaphore_wait(barrier, n + 1)

    left_copy = pltpu.make_async_remote_copy(
        src_ref=left_ref, dst_ref=left, send_sem=left_send, recv_sem=left_recv,
        device_id={"sec": after}, device_id_type=MESH,
    )
    left_copy.start()

    def row_copy(r, o, slot, target):
        return pltpu.make_async_remote_copy(
            src_ref=row.at[r], dst_ref=rows.at[r, slot],
            send_sem=row_send.at[r, o], recv_sem=row_recv.at[r, o],
            device_id={"blk": target}, device_id_type=MESH,
        )

    def exchange(r, sums):
        line = lax.broadcasted_iota(jnp.int32, (8, 128), 0)
        tile = jnp.zeros((8, 128), jnp.float32)
        for i, s in enumerate(sums):
            tile = jnp.where(line == i, s, tile)
        row[r] = tile
        rows[r, me] = tile

        def send(o, carry):
            row_copy(r, o, me, lax.rem(me + o, n)).start()
            return carry

        def take(o, carry):
            row_copy(r, o, lax.rem(me + n - o, n), lax.rem(me + o, n)).wait_recv()
            return carry

        lax.fori_loop(1, n, send, 0)
        lax.fori_loop(1, n, take, 0)
        return rows[r]

    def drain(r):
        def sent(o, carry):
            row_copy(r, o, me, lax.rem(me + o, n)).wait_send()
            return carry

        lax.fori_loop(1, n, sent, 0)

    def dot2(a, b):
        return jnp.sum(jnp.sum(a * b, axis=0), axis=(0, 1), keepdims=True)

    for q in range(blocks):
        d = dims_ref[q]
        inside = (lax.broadcasted_iota(jnp.int32, (side, side), 0) < d) & (
            lax.broadcasted_iota(jnp.int32, (side, side), 1) < d
        )
        mask[q] = inside.astype(jnp.float32)

    psi_load.wait()
    vec_ref[...] = psi_ref[...] * mask[...]
    prev[...] = jnp.zeros_like(prev)
    beta_ref[...] = jnp.zeros_like(beta_ref)

    @pl.when(jnp.logical_not(has_source))
    def _():
        far[...] = jnp.zeros_like(far)

    got = exchange(0, [dot2(vec_ref[...], vec_ref[...])])
    start_sq = jnp.sum(got[:, 0:1, :], axis=0)[:, :1]
    vec_ref[...] = vec_ref[...] * jnp.sqrt(count / start_sq)
    drain(0)
    right_load.wait()

    def step_body(step, carry):
        own[step] = vec_ref[...].astype(jnp.bfloat16)

        def near_copy(c):
            b, r = chunks[c]
            return pltpu.make_async_remote_copy(
                src_ref=own.at[step, b, pl.ds(r, half)], dst_ref=near.at[step, b, pl.ds(r, half)],
                send_sem=near_send.at[step, c], recv_sem=near_recv.at[step, c],
                device_id={"blk": partner}, device_id_type=MESH,
            )

        def far_copy(c):
            b, r = chunks[c]
            return pltpu.make_async_remote_copy(
                src_ref=near.at[step, b, pl.ds(r, half)], dst_ref=far.at[step, b, pl.ds(r, half)],
                send_sem=far_send.at[step, c], recv_sem=far_recv.at[step, c],
                device_id={"blk": target}, device_id_type=MESH,
            )

        for c in range(len(chunks)):
            near_copy(c).start()

        def mix(k, q, block):
            mixed[k, q] = lax.dot_general(
                block, right_ref[k, q], (((1,), (1,)), ((), ())), preferred_element_type=jnp.float32
            ).astype(jnp.bfloat16)

        def term(k, q):
            return jnp.dot(left[k, q], mixed[k, q], preferred_element_type=jnp.float32)

        for q in range(blocks):
            mix(0, q, own[step, q])
            mix(1, q, own[step, q])

        for c in range(len(chunks)):
            near_copy(c).wait_recv()

            @pl.when(has_target)
            def _():
                far_copy(c).start()

        for q in range(blocks):
            mix(3 - odd, q, near[step, q])
        for i in range(blocks - 1):
            mix(5 - odd, i + odd, near[step, i + 1 - odd])

        @pl.when(step == 0)
        def _():
            left_copy.wait()

        for q in range(blocks):
            image[q] = term(0, q) + term(1, q) + term(3 - odd, q)
        for i in range(blocks - 1):
            image[i + odd] += term(5 - odd, i + odd)

        @pl.when(has_source)
        def _():
            for c in range(len(chunks)):
                far_copy(c).wait_recv()

        for q in range(blocks):
            mix(2 + odd, q, far[step, q])
        for i in range(blocks - 1):
            mix(4 + odd, i + 1 - odd, far[step, i + odd])
        for i in range(blocks - 1):
            image[i + 1 - odd] += term(4 + odd, i + 1 - odd)
        for q in range(blocks):
            image[q] = (image[q] + term(2 + odd, q)) * mask[q]

        beta = beta_ref[0:1, 0:1]
        vec = vec_ref[...]
        vw = dot2(vec, image[...])
        vv = dot2(vec, vec)
        image[...] = image[...] - beta * prev[...]
        vt = dot2(vec, image[...])
        mine = vt / jnp.where(vv > 0.0, vv, 1.0)
        rest = image[...] - mine * vec
        got = exchange(step + 1, [vw, mine, vv, dot2(rest, rest), dot2(rest, vec)])
        alpha = jnp.sum(got[:, 0:1, :], axis=0) / count
        gap = got[:, 1:2, :] - alpha[None]
        resid = jnp.sum(got[:, 3:4, :] + 2.0 * gap * got[:, 4:5, :] + gap * gap * got[:, 2:3, :], axis=0)
        next_beta = jnp.sqrt(jnp.maximum(resid, 0.0) / count + 1e-06)
        coef_ref[pl.ds(step, 1)] = alpha
        coef_ref[pl.ds(STEPS + step, 1)] = next_beta
        beta_ref[0:1] = next_beta
        vec = vec_ref[...]
        fresh = (image[...] - alpha[:, :1] * vec) * (1.0 / next_beta[:, :1])
        prev[...] = vec
        vec_ref[...] = fresh
        drain(step + 1)

        for c in range(len(chunks)):
            near_copy(c).wait_send()

        @pl.when(has_target)
        def _():
            for c in range(len(chunks)):
                far_copy(c).wait_send()

        return carry

    lax.fori_loop(0, STEPS, step_body, 0)


def lanczos(left_built, right, psi, dims, n, nsec):
    blocks, side = psi.shape[0], psi.shape[1]
    terms = right.shape[0]
    count = float(n * blocks * side * side)
    vmem = pl.BlockSpec(memory_space=pltpu.VMEM)
    any_place = pl.BlockSpec(memory_space=pl.ANY)
    half = jnp.bfloat16
    return pl.pallas_call(
        functools.partial(lanczos_kernel, n, nsec, count),
        out_shape=(
            jax.ShapeDtypeStruct((blocks, side, side), jnp.float32),
            jax.ShapeDtypeStruct((2 * STEPS, 128), jnp.float32),
        ),
        in_specs=[pl.BlockSpec(memory_space=pltpu.SMEM), any_place, any_place, any_place],
        out_specs=(vmem, vmem),
        scratch_shapes=[
            pltpu.VMEM((terms, blocks, side, side), half),
            pltpu.VMEM((terms, blocks, side, side), half),
            pltpu.VMEM((blocks, side, side), jnp.float32),
            pltpu.VMEM((STEPS, blocks, side, side), half),
            pltpu.VMEM((STEPS, blocks, side, side), half),
            pltpu.VMEM((STEPS, blocks, side, side), half),
            pltpu.VMEM((blocks, side, side), jnp.float32),
            pltpu.VMEM((blocks, side, side), jnp.float32),
            pltpu.VMEM((blocks, side, side), jnp.float32),
            pltpu.VMEM((terms, blocks, side, side), half),
            pltpu.VMEM((STEPS + 1, 8, 128), jnp.float32),
            pltpu.VMEM((STEPS + 1, n, 8, 128), jnp.float32),
            pltpu.VMEM((8, 128), jnp.float32),
            pltpu.SemaphoreType.DMA((2,)),
            pltpu.SemaphoreType.DMA,
            pltpu.SemaphoreType.DMA,
            pltpu.SemaphoreType.DMA((STEPS, 2 * blocks)),
            pltpu.SemaphoreType.DMA((STEPS, 2 * blocks)),
            pltpu.SemaphoreType.DMA((STEPS, 2 * blocks)),
            pltpu.SemaphoreType.DMA((STEPS, 2 * blocks)),
            pltpu.SemaphoreType.DMA((STEPS + 1, n)),
            pltpu.SemaphoreType.DMA((STEPS + 1, n)),
        ],
        compiler_params=pltpu.CompilerParams(
            collective_id=0, has_side_effects=True, vmem_limit_bytes=60 * 1024 * 1024
        ),
        name="lanczos",
    )(dims, left_built, right, psi)


def project_kernel(ranks_ref, vec_ref, sketch_ref, out_ref, gram, side_rows):
    blocks, side, rmax = sketch_ref.shape
    hp = lax.Precision.HIGHEST

    def mul(x, y, dims):
        return lax.dot_general(x, y, (dims, ((), ())), precision=hp, preferred_element_type=jnp.float32)

    line = lax.broadcasted_iota(jnp.int32, (rmax, rmax), 0)
    lane = lax.broadcasted_iota(jnp.int32, (rmax, rmax), 1)
    wide = lax.broadcasted_iota(jnp.int32, (rmax, side), 0)
    for q in range(blocks):
        rank = ranks_ref[q]
        yt = mul(sketch_ref[q], vec_ref[q], ((0,), (1,)))
        yt = jnp.where(wide < rank, yt, 0.0)
        side_rows[q] = yt
        extra = jnp.where((line == lane) & (line >= rank), 1.0, 0.0)
        gram[q] = mul(yt, yt, ((1,), (1,))) + extra
    sub = lax.broadcasted_iota(jnp.int32, (8, 1), 0)
    for p in range(0, rmax, 8):
        g = [gram[q, p : p + 8, :] for q in range(blocks)]
        y = [side_rows[q, p : p + 8, :] for q in range(blocks)]
        scale = [jnp.ones((8, 1), jnp.float32) for q in range(blocks)]
        for j in range(8):
            for q in range(blocks):
                pivot = g[q][j : j + 1, p + j : p + j + 1]
                factor = jnp.where(sub > j, g[q][:, p + j : p + j + 1], 0.0) / pivot
                scale[q] = jnp.where(sub == j, pivot, scale[q])
                y[q] = y[q] - factor * y[q][j : j + 1, :]
                g[q] = g[q] - factor * g[q][j : j + 1, :]
        for q in range(blocks):
            norm = 1.0 / jnp.sqrt(scale[q])
            g[q] = g[q] * norm
            y[q] = y[q] * norm
            side_rows[q, p : p + 8, :] = y[q]
        if p + 8 < rmax:
            flip = [g[q].T for q in range(blocks)]
            for i in range(p + 8, rmax, 8):
                for q in range(blocks):
                    gi = gram[q, i : i + 8, :]
                    yi = side_rows[q, i : i + 8, :]
                    for j in range(8):
                        f = flip[q][i : i + 8, j : j + 1]
                        gi = gi - f * g[q][j : j + 1, :]
                        yi = yi - f * y[q][j : j + 1, :]
                    gram[q, i : i + 8, :] = gi
                    side_rows[q, i : i + 8, :] = yi
    for q in range(blocks):
        z = side_rows[q]
        out_ref[q] = mul(z, mul(z, vec_ref[q], ((1,), (0,))), ((0,), (0,)))


def project(vec, sketch, ranks, **kw):
    blocks, side, rmax = sketch.shape
    vmem = pl.BlockSpec(memory_space=pltpu.VMEM)
    return pl.pallas_call(
        project_kernel,
        out_shape=jax.ShapeDtypeStruct((blocks, side, side), jnp.float32),
        in_specs=[pl.BlockSpec(memory_space=pltpu.SMEM), vmem, vmem],
        out_specs=vmem,
        scratch_shapes=[
            pltpu.VMEM((blocks, rmax, rmax), jnp.float32),
            pltpu.VMEM((blocks, rmax, side), jnp.float32),
        ],
        compiler_params=pltpu.CompilerParams(vmem_limit_bytes=32 * 1024 * 1024),
        name="project",
        **kw,
    )(ranks, vec, sketch)


def shards(left_built, right_env, psi_init, block_dims, ranks, sketch):
    n = lax.axis_size("blk")
    nsec = lax.axis_size("sec")
    vec, coefs = lanczos(left_built[0], right_env[0], psi_init[0], block_dims[0], n, nsec)
    truncated = project(vec, sketch[0], ranks[0])
    return (truncated[None], coefs[:STEPS, 0][None], coefs[STEPS:, 0][None])


def solution(mesh):
    placed = (
        P("sec", None, "blk", None, None),
        P("sec", None, "blk", None, None),
        P("sec", "blk", None, None),
        P("sec", "blk"),
        P("sec", "blk"),
        P("sec", "blk", None, None),
    )
    return jax.shard_map(
        shards,
        mesh=mesh,
        in_specs=placed,
        out_specs=(P("sec", "blk", None, None), P("sec", None), P("sec", None)),
        check_vma=False,
    )
```

```python
import functools

import jax
import jax.numpy as jnp
from jax import lax
from jax.experimental import pallas as pl
from jax.experimental.pallas import tpu as pltpu
from jax.sharding import PartitionSpec as P

STEPS = 4
MESH = pl.DeviceIdType.MESH


def lanczos_kernel(
    n, nsec, count, dims_ref, left_ref, right_hbm, psi_hbm, vec_ref, coef_ref,
    left, right_ref, psi_ref, own, near, far, prev, image, mask, mixed, row, rows, beta_ref,
    load, left_send, left_recv, near_send, near_recv, far_send, far_recv, row_send, row_recv,
):
    blocks, side = psi_ref.shape[0], psi_ref.shape[1]
    terms = right_ref.shape[0]
    me = lax.axis_index("blk")
    sec = lax.axis_index("sec")
    after = lax.rem(sec + 1, nsec)
    before = lax.rem(sec + nsec - 1, nsec)

    odd = lax.rem(me, 2)
    partner = me + 1 - 2 * odd
    target = me + 2 - 4 * odd
    source = me - 2 + 4 * odd
    has_target = (target >= 0) & (target < n)
    has_source = (source >= 0) & (source < n)
    half = side // 2
    chunks = [(b, h * half) for b in range(blocks) for h in range(2)]

    psi_load = pltpu.make_async_copy(psi_hbm, psi_ref, load.at[0])
    right_load = pltpu.make_async_copy(right_hbm, right_ref, load.at[1])
    psi_load.start()
    right_load.start()

    barrier = pltpu.get_barrier_semaphore()

    def greet(o, carry):
        pl.semaphore_signal(barrier, inc=1, device_id={"blk": lax.rem(me + o, n)}, device_id_type=MESH)
        return carry

    lax.fori_loop(1, n, greet, 0)
    for other in (after, before):
        pl.semaphore_signal(barrier, inc=1, device_id={"sec": other}, device_id_type=MESH)
    pl.semaphore_wait(barrier, n + 1)

    order = [0, 1, 3 - odd, 5 - odd, 2 + odd, 4 + odd]

    def left_copy(i):
        return pltpu.make_async_remote_copy(
            src_ref=left_ref.at[order[i]], dst_ref=left.at[order[i]],
            send_sem=left_send.at[i], recv_sem=left_recv.at[i],
            device_id={"sec": after}, device_id_type=MESH,
        )

    for i in range(len(order)):
        left_copy(i).start()

    def row_copy(r, o, slot, target):
        return pltpu.make_async_remote_copy(
            src_ref=row.at[r], dst_ref=rows.at[r, slot],
            send_sem=row_send.at[r, o], recv_sem=row_recv.at[r, o],
            device_id={"blk": target}, device_id_type=MESH,
        )

    def exchange(r, sums):
        line = lax.broadcasted_iota(jnp.int32, (8, 128), 0)
        tile = jnp.zeros((8, 128), jnp.float32)
        for i, s in enumerate(sums):
            tile = jnp.where(line == i, s, tile)
        row[r] = tile
        rows[r, me] = tile

        def send(o, carry):
            row_copy(r, o, me, lax.rem(me + o, n)).start()
            return carry

        def take(o, carry):
            row_copy(r, o, lax.rem(me + n - o, n), lax.rem(me + o, n)).wait_recv()
            return carry

        lax.fori_loop(1, n, send, 0)
        lax.fori_loop(1, n, take, 0)
        return rows[r]

    def drain(r):
        def sent(o, carry):
            row_copy(r, o, me, lax.rem(me + o, n)).wait_send()
            return carry

        lax.fori_loop(1, n, sent, 0)

    def dot2(a, b):
        return jnp.sum(jnp.sum(a * b, axis=0), axis=(0, 1), keepdims=True)

    for q in range(blocks):
        d = dims_ref[q]
        inside = (lax.broadcasted_iota(jnp.int32, (side, side), 0) < d) & (
            lax.broadcasted_iota(jnp.int32, (side, side), 1) < d
        )
        mask[q] = inside.astype(jnp.float32)

    psi_load.wait()
    vec_ref[...] = psi_ref[...] * mask[...]
    prev[...] = jnp.zeros_like(prev)
    beta_ref[...] = jnp.zeros_like(beta_ref)

    @pl.when(jnp.logical_not(has_source))
    def _():
        far[...] = jnp.zeros_like(far)

    got = exchange(0, [dot2(vec_ref[...], vec_ref[...])])
    start_sq = jnp.sum(got[:, 0:1, :], axis=0)[:, :1]
    vec_ref[...] = vec_ref[...] * jnp.sqrt(count / start_sq)
    drain(0)
    right_load.wait()

    def step_body(step, carry):
        own[step] = vec_ref[...].astype(jnp.bfloat16)

        def near_copy(c):
            b, r = chunks[c]
            return pltpu.make_async_remote_copy(
                src_ref=own.at[step, b, pl.ds(r, half)], dst_ref=near.at[step, b, pl.ds(r, half)],
                send_sem=near_send.at[step, c], recv_sem=near_recv.at[step, c],
                device_id={"blk": partner}, device_id_type=MESH,
            )

        def far_copy(c):
            b, r = chunks[c]
            return pltpu.make_async_remote_copy(
                src_ref=near.at[step, b, pl.ds(r, half)], dst_ref=far.at[step, b, pl.ds(r, half)],
                send_sem=far_send.at[step, c], recv_sem=far_recv.at[step, c],
                device_id={"blk": target}, device_id_type=MESH,
            )

        for c in range(len(chunks)):
            near_copy(c).start()

        def mix(k, q, block):
            mixed[k, q] = lax.dot_general(
                block, right_ref[k, q], (((1,), (1,)), ((), ())), preferred_element_type=jnp.float32
            ).astype(jnp.bfloat16)

        def term(k, q):
            return jnp.dot(left[k, q], mixed[k, q], preferred_element_type=jnp.float32)

        for q in range(blocks):
            mix(0, q, own[step, q])
            mix(1, q, own[step, q])

        def apply_own():
            for q in range(blocks):
                image[q] = term(0, q) + term(1, q)

        def left_wait(terms_of):
            @pl.when(step == 0)
            def _():
                for i in terms_of:
                    left_copy(i).wait()

        pl.when(step > 0)(apply_own)

        for c in range(len(chunks)):
            near_copy(c).wait_recv()

            @pl.when(has_target)
            def _():
                far_copy(c).start()

        for q in range(blocks):
            mix(3 - odd, q, near[step, q])
        for i in range(blocks - 1):
            mix(5 - odd, i + odd, near[step, i + 1 - odd])

        left_wait((0, 1))
        pl.when(step == 0)(apply_own)
        left_wait((2, 3))
        for q in range(blocks):
            image[q] += term(3 - odd, q)
        for i in range(blocks - 1):
            image[i + odd] += term(5 - odd, i + odd)

        @pl.when(has_source)
        def _():
            for c in range(len(chunks)):
                far_copy(c).wait_recv()

        for q in range(blocks):
            mix(2 + odd, q, far[step, q])
        for i in range(blocks - 1):
            mix(4 + odd, i + 1 - odd, far[step, i + odd])
        left_wait((4, 5))
        for i in range(blocks - 1):
            image[i + 1 - odd] += term(4 + odd, i + 1 - odd)
        for q in range(blocks):
            image[q] = (image[q] + term(2 + odd, q)) * mask[q]

        beta = beta_ref[0:1, 0:1]
        vec = vec_ref[...]
        vw = dot2(vec, image[...])
        vv = dot2(vec, vec)
        image[...] = image[...] - beta * prev[...]
        vt = dot2(vec, image[...])
        mine = vt / jnp.where(vv > 0.0, vv, 1.0)
        rest = image[...] - mine * vec
        got = exchange(step + 1, [vw, mine, vv, dot2(rest, rest), dot2(rest, vec)])
        alpha = jnp.sum(got[:, 0:1, :], axis=0) / count
        gap = got[:, 1:2, :] - alpha[None]
        resid = jnp.sum(got[:, 3:4, :] + 2.0 * gap * got[:, 4:5, :] + gap * gap * got[:, 2:3, :], axis=0)
        next_beta = jnp.sqrt(jnp.maximum(resid, 0.0) / count + 1e-06)
        coef_ref[pl.ds(step, 1)] = alpha
        coef_ref[pl.ds(STEPS + step, 1)] = next_beta
        beta_ref[0:1] = next_beta
        vec = vec_ref[...]
        fresh = (image[...] - alpha[:, :1] * vec) * (1.0 / next_beta[:, :1])
        prev[...] = vec
        vec_ref[...] = fresh
        drain(step + 1)

        for c in range(len(chunks)):
            near_copy(c).wait_send()

        @pl.when(has_target)
        def _():
            for c in range(len(chunks)):
                far_copy(c).wait_send()

        return carry

    lax.fori_loop(0, STEPS, step_body, 0)


def lanczos(left_built, right, psi, dims, n, nsec):
    blocks, side = psi.shape[0], psi.shape[1]
    terms = right.shape[0]
    count = float(n * blocks * side * side)
    vmem = pl.BlockSpec(memory_space=pltpu.VMEM)
    any_place = pl.BlockSpec(memory_space=pl.ANY)
    half = jnp.bfloat16
    return pl.pallas_call(
        functools.partial(lanczos_kernel, n, nsec, count),
        out_shape=(
            jax.ShapeDtypeStruct((blocks, side, side), jnp.float32),
            jax.ShapeDtypeStruct((2 * STEPS, 128), jnp.float32),
        ),
        in_specs=[pl.BlockSpec(memory_space=pltpu.SMEM), any_place, any_place, any_place],
        out_specs=(vmem, vmem),
        scratch_shapes=[
            pltpu.VMEM((terms, blocks, side, side), half),
            pltpu.VMEM((terms, blocks, side, side), half),
            pltpu.VMEM((blocks, side, side), jnp.float32),
            pltpu.VMEM((STEPS, blocks, side, side), half),
            pltpu.VMEM((STEPS, blocks, side, side), half),
            pltpu.VMEM((STEPS, blocks, side, side), half),
            pltpu.VMEM((blocks, side, side), jnp.float32),
            pltpu.VMEM((blocks, side, side), jnp.float32),
            pltpu.VMEM((blocks, side, side), jnp.float32),
            pltpu.VMEM((terms, blocks, side, side), half),
            pltpu.VMEM((STEPS + 1, 8, 128), jnp.float32),
            pltpu.VMEM((STEPS + 1, n, 8, 128), jnp.float32),
            pltpu.VMEM((8, 128), jnp.float32),
            pltpu.SemaphoreType.DMA((2,)),
            pltpu.SemaphoreType.DMA((terms,)),
            pltpu.SemaphoreType.DMA((terms,)),
            pltpu.SemaphoreType.DMA((STEPS, 2 * blocks)),
            pltpu.SemaphoreType.DMA((STEPS, 2 * blocks)),
            pltpu.SemaphoreType.DMA((STEPS, 2 * blocks)),
            pltpu.SemaphoreType.DMA((STEPS, 2 * blocks)),
            pltpu.SemaphoreType.DMA((STEPS + 1, n)),
            pltpu.SemaphoreType.DMA((STEPS + 1, n)),
        ],
        compiler_params=pltpu.CompilerParams(
            collective_id=0, has_side_effects=True, vmem_limit_bytes=60 * 1024 * 1024
        ),
        name="lanczos",
    )(dims, left_built, right, psi)


def project_kernel(ranks_ref, vec_ref, sketch_ref, out_ref, gram, side_rows):
    blocks, side, rmax = sketch_ref.shape
    hp = lax.Precision.HIGHEST

    def mul(x, y, dims):
        return lax.dot_general(x, y, (dims, ((), ())), precision=hp, preferred_element_type=jnp.float32)

    line = lax.broadcasted_iota(jnp.int32, (rmax, rmax), 0)
    lane = lax.broadcasted_iota(jnp.int32, (rmax, rmax), 1)
    wide = lax.broadcasted_iota(jnp.int32, (rmax, side), 0)
    for q in range(blocks):
        rank = ranks_ref[q]
        yt = mul(sketch_ref[q], vec_ref[q], ((0,), (1,)))
        yt = jnp.where(wide < rank, yt, 0.0)
        side_rows[q] = yt
        extra = jnp.where((line == lane) & (line >= rank), 1.0, 0.0)
        gram[q] = mul(yt, yt, ((1,), (1,))) + extra
    sub = lax.broadcasted_iota(jnp.int32, (8, rmax), 0)
    for p in range(0, rmax, 8):
        g = [gram[q, p : p + 8, :] for q in range(blocks)]
        y = [side_rows[q, p : p + 8, :] for q in range(blocks)]
        scale = [jnp.ones((8, rmax), jnp.float32) for q in range(blocks)]
        for j in range(8):
            for q in range(blocks):
                column = jnp.broadcast_to(g[q][:, p + j : p + j + 1], (8, rmax))
                pivot = jnp.broadcast_to(column[j : j + 1, :], (8, rmax))
                factor = jnp.where(sub > j, column, 0.0) * (1.0 / pivot)
                scale[q] = jnp.where(sub == j, pivot, scale[q])
                wide_factor = jnp.concatenate([factor] * (side // rmax), axis=1)
                y[q] = y[q] - wide_factor * y[q][j : j + 1, :]
                g[q] = g[q] - factor * g[q][j : j + 1, :]
        for q in range(blocks):
            norm = 1.0 / jnp.sqrt(scale[q])
            g[q] = g[q] * norm
            y[q] = y[q] * jnp.concatenate([norm] * (side // rmax), axis=1)
            side_rows[q, p : p + 8, :] = y[q]
        if p + 8 < rmax:
            flip = [g[q].T for q in range(blocks)]
            for i in range(p + 8, rmax, 8):
                for q in range(blocks):
                    gi = gram[q, i : i + 8, :]
                    yi = side_rows[q, i : i + 8, :]
                    for j in range(8):
                        f = flip[q][i : i + 8, j : j + 1]
                        gi = gi - f * g[q][j : j + 1, :]
                        yi = yi - f * y[q][j : j + 1, :]
                    gram[q, i : i + 8, :] = gi
                    side_rows[q, i : i + 8, :] = yi
    for q in range(blocks):
        z = side_rows[q]
        out_ref[q] = mul(z, mul(z, vec_ref[q], ((1,), (0,))), ((0,), (0,)))


def project(vec, sketch, ranks, **kw):
    blocks, side, rmax = sketch.shape
    vmem = pl.BlockSpec(memory_space=pltpu.VMEM)
    return pl.pallas_call(
        project_kernel,
        out_shape=jax.ShapeDtypeStruct((blocks, side, side), jnp.float32),
        in_specs=[pl.BlockSpec(memory_space=pltpu.SMEM), vmem, vmem],
        out_specs=vmem,
        scratch_shapes=[
            pltpu.VMEM((blocks, rmax, rmax), jnp.float32),
            pltpu.VMEM((blocks, rmax, side), jnp.float32),
        ],
        compiler_params=pltpu.CompilerParams(vmem_limit_bytes=32 * 1024 * 1024),
        name="project",
        **kw,
    )(ranks, vec, sketch)


def shards(left_built, right_env, psi_init, block_dims, ranks, sketch):
    n = lax.axis_size("blk")
    nsec = lax.axis_size("sec")
    vec, coefs = lanczos(left_built[0], right_env[0], psi_init[0], block_dims[0], n, nsec)
    truncated = project(vec, sketch[0], ranks[0])
    return (truncated[None], coefs[:STEPS, 0][None], coefs[STEPS:, 0][None])


def solution(mesh):
    placed = (
        P("sec", None, "blk", None, None),
        P("sec", None, "blk", None, None),
        P("sec", "blk", None, None),
        P("sec", "blk"),
        P("sec", "blk"),
        P("sec", "blk", None, None),
    )
    return jax.shard_map(
        shards,
        mesh=mesh,
        in_specs=placed,
        out_specs=(P("sec", "blk", None, None), P("sec", None), P("sec", None)),
        check_vma=False,
    )
```

```python
import functools

import jax
import jax.numpy as jnp
from jax import lax
from jax.experimental import pallas as pl
from jax.experimental.pallas import tpu as pltpu
from jax.sharding import PartitionSpec as P

STEPS = 4
MESH = pl.DeviceIdType.MESH


def lanczos_kernel(
    n, nsec, count, dims_ref, left_ref, right_hbm, psi_hbm, vec_ref, coef_ref,
    left, right_ref, psi_ref, own, near, far, prev, image, mask, mixed, row, rows, beta_ref,
    load, left_send, left_recv, near_send, near_recv, far_send, far_recv, row_send, row_recv,
):
    blocks, side = psi_ref.shape[0], psi_ref.shape[1]
    terms = right_ref.shape[0]
    me = lax.axis_index("blk")
    sec = lax.axis_index("sec")
    after = lax.rem(sec + 1, nsec)
    before = lax.rem(sec + nsec - 1, nsec)

    odd = lax.rem(me, 2)
    partner = me + 1 - 2 * odd
    target = me + 2 - 4 * odd
    source = me - 2 + 4 * odd
    has_target = (target >= 0) & (target < n)
    has_source = (source >= 0) & (source < n)
    half = side // 2
    chunks = [(b, h * half) for b in range(blocks) for h in range(2)]

    psi_load = pltpu.make_async_copy(psi_hbm, psi_ref, load.at[0])
    right_load = pltpu.make_async_copy(right_hbm, right_ref, load.at[1])
    psi_load.start()
    right_load.start()

    barrier = pltpu.get_barrier_semaphore()

    def greet(o, carry):
        pl.semaphore_signal(barrier, inc=1, device_id={"blk": lax.rem(me + o, n)}, device_id_type=MESH)
        return carry

    lax.fori_loop(1, n, greet, 0)
    for other in (after, before):
        pl.semaphore_signal(barrier, inc=1, device_id={"sec": other}, device_id_type=MESH)
    pl.semaphore_wait(barrier, n + 1)

    order = [0, 1, 3 - odd, 5 - odd, 2 + odd, 4 + odd]

    def left_copy(i):
        return pltpu.make_async_remote_copy(
            src_ref=left_ref.at[order[i]], dst_ref=left.at[order[i]],
            send_sem=left_send.at[i], recv_sem=left_recv.at[i],
            device_id={"sec": after}, device_id_type=MESH,
        )

    for i in range(len(order)):
        left_copy(i).start()

    def row_copy(r, o, slot, target):
        return pltpu.make_async_remote_copy(
            src_ref=row.at[r], dst_ref=rows.at[r, slot],
            send_sem=row_send.at[r, o], recv_sem=row_recv.at[r, o],
            device_id={"blk": target}, device_id_type=MESH,
        )

    def exchange(r, sums):
        line = lax.broadcasted_iota(jnp.int32, (8, 128), 0)
        tile = jnp.zeros((8, 128), jnp.float32)
        for i, s in enumerate(sums):
            tile = jnp.where(line == i, s, tile)
        row[r] = tile
        rows[r, me] = tile

        def send(o, carry):
            row_copy(r, o, me, lax.rem(me + o, n)).start()
            return carry

        def take(o, carry):
            row_copy(r, o, lax.rem(me + n - o, n), lax.rem(me + o, n)).wait_recv()
            return carry

        lax.fori_loop(1, n, send, 0)
        lax.fori_loop(1, n, take, 0)
        return rows[r]

    def drain(r):
        def sent(o, carry):
            row_copy(r, o, me, lax.rem(me + o, n)).wait_send()
            return carry

        lax.fori_loop(1, n, sent, 0)

    def dot2(a, b):
        return jnp.sum(jnp.sum(a * b, axis=0), axis=(0, 1), keepdims=True)

    for q in range(blocks):
        d = dims_ref[q]
        inside = (lax.broadcasted_iota(jnp.int32, (side, side), 0) < d) & (
            lax.broadcasted_iota(jnp.int32, (side, side), 1) < d
        )
        mask[q] = inside.astype(jnp.float32)

    psi_load.wait()
    vec_ref[...] = psi_ref[...] * mask[...]
    prev[...] = jnp.zeros_like(prev)
    beta_ref[...] = jnp.zeros_like(beta_ref)

    @pl.when(jnp.logical_not(has_source))
    def _():
        far[...] = jnp.zeros_like(far)

    got = exchange(0, [dot2(vec_ref[...], vec_ref[...])])
    start_sq = jnp.sum(got[:, 0:1, :], axis=0)[:, :1]
    vec_ref[...] = vec_ref[...] * jnp.sqrt(count / start_sq)
    drain(0)
    right_load.wait()

    def step_body(step, carry):
        own[step] = vec_ref[...].astype(jnp.bfloat16)

        def near_copy(c):
            b, r = chunks[c]
            return pltpu.make_async_remote_copy(
                src_ref=own.at[step, b, pl.ds(r, half)], dst_ref=near.at[step, b, pl.ds(r, half)],
                send_sem=near_send.at[step, c], recv_sem=near_recv.at[step, c],
                device_id={"blk": partner}, device_id_type=MESH,
            )

        def far_copy(c):
            b, r = chunks[c]
            return pltpu.make_async_remote_copy(
                src_ref=near.at[step, b, pl.ds(r, half)], dst_ref=far.at[step, b, pl.ds(r, half)],
                send_sem=far_send.at[step, c], recv_sem=far_recv.at[step, c],
                device_id={"blk": target}, device_id_type=MESH,
            )

        for c in range(len(chunks)):
            near_copy(c).start()

        def mix(k, q, block):
            mixed[k, q] = lax.dot_general(
                block, right_ref[k, q], (((1,), (1,)), ((), ())), preferred_element_type=jnp.float32
            ).astype(jnp.bfloat16)

        def term(k, q):
            return jnp.dot(left[k, q], mixed[k, q], preferred_element_type=jnp.float32)

        for q in range(blocks):
            mix(0, q, own[step, q])
            mix(1, q, own[step, q])

        def apply_own():
            for q in range(blocks):
                image[q] = term(0, q) + term(1, q)

        def left_wait(terms_of):
            @pl.when(step == 0)
            def _():
                for i in terms_of:
                    left_copy(i).wait()

        pl.when(step > 0)(apply_own)

        for c in range(len(chunks)):
            near_copy(c).wait_recv()

            @pl.when(has_target)
            def _():
                far_copy(c).start()

        for q in range(blocks):
            mix(3 - odd, q, near[step, q])
        for i in range(blocks - 1):
            mix(5 - odd, i + odd, near[step, i + 1 - odd])

        left_wait((0, 1))
        pl.when(step == 0)(apply_own)
        left_wait((2, 3))
        for q in range(blocks):
            image[q] += term(3 - odd, q)
        for i in range(blocks - 1):
            image[i + odd] += term(5 - odd, i + odd)

        @pl.when(has_source)
        def _():
            for c in range(len(chunks)):
                far_copy(c).wait_recv()

        for q in range(blocks):
            mix(2 + odd, q, far[step, q])
        for i in range(blocks - 1):
            mix(4 + odd, i + 1 - odd, far[step, i + odd])
        left_wait((4, 5))
        for i in range(blocks - 1):
            image[i + 1 - odd] += term(4 + odd, i + 1 - odd)
        for q in range(blocks):
            image[q] = (image[q] + term(2 + odd, q)) * mask[q]

        beta = beta_ref[0:1, 0:1]
        vec = vec_ref[...]
        vw = dot2(vec, image[...])
        vv = dot2(vec, vec)
        image[...] = image[...] - beta * prev[...]
        vt = dot2(vec, image[...])
        mine = vt / jnp.where(vv > 0.0, vv, 1.0)
        rest = image[...] - mine * vec
        got = exchange(step + 1, [vw, mine, vv, dot2(rest, rest), dot2(rest, vec)])
        alpha = jnp.sum(got[:, 0:1, :], axis=0) / count
        gap = got[:, 1:2, :] - alpha[None]
        resid = jnp.sum(got[:, 3:4, :] + 2.0 * gap * got[:, 4:5, :] + gap * gap * got[:, 2:3, :], axis=0)
        next_beta = jnp.sqrt(jnp.maximum(resid, 0.0) / count + 1e-06)
        coef_ref[pl.ds(step, 1)] = alpha
        coef_ref[pl.ds(STEPS + step, 1)] = next_beta
        beta_ref[0:1] = next_beta
        vec = vec_ref[...]
        fresh = (image[...] - alpha[:, :1] * vec) * (1.0 / next_beta[:, :1])
        prev[...] = vec
        vec_ref[...] = fresh
        drain(step + 1)

        for c in range(len(chunks)):
            near_copy(c).wait_send()

        @pl.when(has_target)
        def _():
            for c in range(len(chunks)):
                far_copy(c).wait_send()

        return carry

    lax.fori_loop(0, STEPS, step_body, 0)


def lanczos(left_built, right, psi, dims, n, nsec):
    blocks, side = psi.shape[0], psi.shape[1]
    terms = right.shape[0]
    count = float(n * blocks * side * side)
    vmem = pl.BlockSpec(memory_space=pltpu.VMEM)
    any_place = pl.BlockSpec(memory_space=pl.ANY)
    half = jnp.bfloat16
    return pl.pallas_call(
        functools.partial(lanczos_kernel, n, nsec, count),
        out_shape=(
            jax.ShapeDtypeStruct((blocks, side, side), jnp.float32),
            jax.ShapeDtypeStruct((2 * STEPS, 128), jnp.float32),
        ),
        in_specs=[pl.BlockSpec(memory_space=pltpu.SMEM), any_place, any_place, any_place],
        out_specs=(vmem, vmem),
        scratch_shapes=[
            pltpu.VMEM((terms, blocks, side, side), half),
            pltpu.VMEM((terms, blocks, side, side), half),
            pltpu.VMEM((blocks, side, side), jnp.float32),
            pltpu.VMEM((STEPS, blocks, side, side), half),
            pltpu.VMEM((STEPS, blocks, side, side), half),
            pltpu.VMEM((STEPS, blocks, side, side), half),
            pltpu.VMEM((blocks, side, side), jnp.float32),
            pltpu.VMEM((blocks, side, side), jnp.float32),
            pltpu.VMEM((blocks, side, side), jnp.float32),
            pltpu.VMEM((terms, blocks, side, side), half),
            pltpu.VMEM((STEPS + 1, 8, 128), jnp.float32),
            pltpu.VMEM((STEPS + 1, n, 8, 128), jnp.float32),
            pltpu.VMEM((8, 128), jnp.float32),
            pltpu.SemaphoreType.DMA((2,)),
            pltpu.SemaphoreType.DMA((terms,)),
            pltpu.SemaphoreType.DMA((terms,)),
            pltpu.SemaphoreType.DMA((STEPS, 2 * blocks)),
            pltpu.SemaphoreType.DMA((STEPS, 2 * blocks)),
            pltpu.SemaphoreType.DMA((STEPS, 2 * blocks)),
            pltpu.SemaphoreType.DMA((STEPS, 2 * blocks)),
            pltpu.SemaphoreType.DMA((STEPS + 1, n)),
            pltpu.SemaphoreType.DMA((STEPS + 1, n)),
        ],
        compiler_params=pltpu.CompilerParams(
            collective_id=0, has_side_effects=True, vmem_limit_bytes=60 * 1024 * 1024
        ),
        name="lanczos",
    )(dims, left_built, right, psi)


def project_kernel(ranks_ref, vec_ref, sketch_ref, out_ref, gram, side_rows):
    blocks, side, rmax = sketch_ref.shape
    hp = lax.Precision.HIGHEST

    def mul(x, y, dims):
        return lax.dot_general(x, y, (dims, ((), ())), precision=hp, preferred_element_type=jnp.float32)

    line = lax.broadcasted_iota(jnp.int32, (rmax, rmax), 0)
    lane = lax.broadcasted_iota(jnp.int32, (rmax, rmax), 1)
    wide = lax.broadcasted_iota(jnp.int32, (rmax, side), 0)
    for q in range(blocks):
        rank = ranks_ref[q]
        yt = mul(sketch_ref[q], vec_ref[q], ((0,), (1,)))
        yt = jnp.where(wide < rank, yt, 0.0)
        side_rows[q] = yt
        extra = jnp.where((line == lane) & (line >= rank), 1.0, 0.0)
        gram[q] = mul(yt, yt, ((1,), (1,))) + extra
    sub = lax.broadcasted_iota(jnp.int32, (8, 1), 0)
    for p in range(0, rmax, 8):
        g = [gram[q, p : p + 8, :] for q in range(blocks)]
        y = [side_rows[q, p : p + 8, :] for q in range(blocks)]
        scale = [jnp.ones((8, 1), jnp.float32) for q in range(blocks)]
        for j in range(8):
            for q in range(blocks):
                pivot = g[q][j : j + 1, p + j : p + j + 1]
                factor = jnp.where(sub > j, g[q][:, p + j : p + j + 1], 0.0) / pivot
                scale[q] = jnp.where(sub == j, pivot, scale[q])
                y[q] = y[q] - factor * y[q][j : j + 1, :]
                g[q] = g[q] - factor * g[q][j : j + 1, :]
        for q in range(blocks):
            norm = 1.0 / jnp.sqrt(scale[q])
            g[q] = g[q] * norm
            y[q] = y[q] * norm
            side_rows[q, p : p + 8, :] = y[q]
        if p + 8 < rmax:
            flip = [g[q].T for q in range(blocks)]
            for i in range(p + 8, rmax, 8):
                for q in range(blocks):
                    gi = gram[q, i : i + 8, :]
                    yi = side_rows[q, i : i + 8, :]
                    for j in range(8):
                        f = flip[q][i : i + 8, j : j + 1]
                        gi = gi - f * g[q][j : j + 1, :]
                        yi = yi - f * y[q][j : j + 1, :]
                    gram[q, i : i + 8, :] = gi
                    side_rows[q, i : i + 8, :] = yi
    for q in range(blocks):
        z = side_rows[q]
        out_ref[q] = mul(z, mul(z, vec_ref[q], ((1,), (0,))), ((0,), (0,)))


def project(vec, sketch, ranks, **kw):
    blocks, side, rmax = sketch.shape
    vmem = pl.BlockSpec(memory_space=pltpu.VMEM)
    return pl.pallas_call(
        project_kernel,
        out_shape=jax.ShapeDtypeStruct((blocks, side, side), jnp.float32),
        in_specs=[pl.BlockSpec(memory_space=pltpu.SMEM), vmem, vmem],
        out_specs=vmem,
        scratch_shapes=[
            pltpu.VMEM((blocks, rmax, rmax), jnp.float32),
            pltpu.VMEM((blocks, rmax, side), jnp.float32),
        ],
        compiler_params=pltpu.CompilerParams(vmem_limit_bytes=32 * 1024 * 1024),
        name="project",
        **kw,
    )(ranks, vec, sketch)


def shards(left_built, right_env, psi_init, block_dims, ranks, sketch):
    n = lax.axis_size("blk")
    nsec = lax.axis_size("sec")
    vec, coefs = lanczos(left_built[0], right_env[0], psi_init[0], block_dims[0], n, nsec)
    truncated = project(vec, sketch[0], ranks[0])
    return (truncated[None], coefs[:STEPS, 0][None], coefs[STEPS:, 0][None])


def solution(mesh):
    placed = (
        P("sec", None, "blk", None, None),
        P("sec", None, "blk", None, None),
        P("sec", "blk", None, None),
        P("sec", "blk"),
        P("sec", "blk"),
        P("sec", "blk", None, None),
    )
    return jax.shard_map(
        shards,
        mesh=mesh,
        in_specs=placed,
        out_specs=(P("sec", "blk", None, None), P("sec", None), P("sec", None)),
        check_vma=False,
    )
```
